32 devices in a mesh: blocks: 2 (over y), sec: 8 (over z, x), pln: 2 (over core).
Axes of the slice: x: 2, y: 2, z: 4, core: 2. Of those that a mesh axis runs over, the one named last changes fastest.
Arguments:
- section_tiles: float32 [16, 256, 512], P(('blocks', 'sec'), 'pln'), parts along dimension 0, may hold values from -6 to 6
Outputs:
- flow_scores: float32 [16, 4, 8, 4096], P(('blocks', 'sec'), 'pln'), parts along dimension 0
The draws below stay inside these ranges and needn't reach their ends.
There are 2 independent parts, one for each index of `blocks`. The reference program is written for one: setup_inputs(seed, part) draws one part's arguments, and reference() takes and returns one part's arrays. A program takes and returns all parts, laid end to end along the dimension named above; each array names one. Nothing has to cross between parts.
All inputs are finite; a program needn't handle non-finite values.
Results may differ from the reference program's by a relative error of at most 0.0003.
Values sent between devices are 32-bit elements; how exact they have to be, the bound alone decides.
No kernel may reach another device: no remote copies, remote signals or barrier semaphores. Data moves between devices by JAX's collectives and lax.ppermute only.
A program may use at most 64 MiB of HBM per device.

```python
import jax
import jax.numpy as jnp
from jax import lax

COLS = 512
PATCH = 128
STRIDE = 64
CROP = 64
MARGIN = 32
NSEC = 8
HEIGHT = 256


def levels(own_key, shape, shards, smallest, high):
    gain, own = 1.0, jax.random.fold_in(own_key, 6)
    for dim, shards_of in shards:
        heights = jnp.exp(jax.random.uniform(jax.random.fold_in(own, dim), (shards_of,), jnp.float32, smallest / len(shards), high / len(shards)))
        gain = gain * jnp.repeat(heights, shape[dim] // shards_of).reshape([-1 if axis == dim else 1 for axis in range(len(shape))])
    return gain


def bell_draw(key, shape, spread, reach, split=(), kind=jnp.bfloat16):
    drawn = spread * jax.random.normal(key, shape, jnp.float32)
    if split:
        drawn = drawn * levels(key, shape, split, -0.22, 0.18)
    return jnp.clip(drawn, -reach, reach).astype(kind)


def setup_inputs(seed: int = 0, part: int = 0) -> dict:
    arg_keys = jax.random.split(jax.random.key(seed), 2)
    part_splits = jax.random.split(jax.random.fold_in(arg_keys[1], part), 2)
    return {
        "section_tiles": bell_draw(part_splits[0], (NSEC, HEIGHT, COLS), 1.0, 6.0, ((0, 8), (1, 2)), jnp.float32),
    }


def patch_stack(section_image):
    padded = jnp.pad(section_image, ((MARGIN, MARGIN), (MARGIN, MARGIN)))
    grid_rows = section_image.shape[0] // STRIDE
    grid_cols = section_image.shape[1] // STRIDE
    blocks = padded.reshape(grid_rows + 1, STRIDE, grid_cols + 1, STRIDE)
    blocks = blocks.transpose(0, 2, 1, 3)
    upper_half = jnp.concatenate([blocks[:-1, :-1], blocks[:-1, 1:]], axis=3)
    lower_half = jnp.concatenate([blocks[1:, :-1], blocks[1:, 1:]], axis=3)
    return jnp.concatenate([upper_half, lower_half], axis=2)


def section_scores(section_tiles, section_index):
    def spectrum(distance):
        source = jnp.maximum(section_index - distance, 0).astype(jnp.int32)
        picked = lax.dynamic_index_in_dim(section_tiles, source, 0, keepdims=False)
        present = section_index >= distance
        picked = jnp.where(present, picked, jnp.zeros_like(picked))
        return jnp.fft.fft2(patch_stack(picked))

    own_spec = spectrum(0)
    crop_start = PATCH // 2 - CROP // 2
    surfaces = []
    for distance in (1, 2):
        earlier_spec = spectrum(distance)
        circular = jnp.fft.ifft2(own_spec * jnp.conj(earlier_spec)).real
        circular = jnp.fft.fftshift(circular, axes=(2, 3))
        cropped = circular[:, :, crop_start:crop_start + CROP, crop_start:crop_start + CROP] / PATCH
        surfaces.append(cropped)
    consensus = surfaces[0] + surfaces[1] + surfaces[0] * surfaces[1]
    return consensus.reshape(consensus.shape[0], consensus.shape[1], CROP * CROP)


def reference(section_tiles):
    indices = jnp.arange(section_tiles.shape[0], dtype=jnp.int32)
    consensus = lax.map(lambda section_index: section_scores(section_tiles, section_index), indices)
    padded = jnp.pad(consensus, ((0, 0), (1, 1), (1, 1), (0, 0)))
    rows_mix = padded[:, :-2] + 2.0 * padded[:, 1:-1] + padded[:, 2:]
    mixed = rows_mix[:, :, :-2] + 2.0 * rows_mix[:, :, 1:-1] + rows_mix[:, :, 2:]
    return mixed / 16.0
```

```python
import functools

import jax
import jax.numpy as jnp
import numpy as np
from jax import lax
from jax.experimental import pallas as pl
from jax.experimental.pallas import tpu as pltpu
from jax.sharding import PartitionSpec as P

PATCH = 128
STRIDE = 64
CROP = 64
MARGIN = 32
HALF = PATCH // 2
LANES = 128
PAIRS = CROP // 2
NYQ = 16

BF16 = jnp.bfloat16
F32 = jnp.float32


def high_low(table):
    table = np.asarray(table, np.float32)
    high = table.astype(jnp.bfloat16)
    low = (table - high.astype(np.float32)).astype(jnp.bfloat16)
    return high, low


def tables():
    turn = 2.0 * np.pi / PATCH
    freq, place, full = np.arange(HALF), np.arange(PATCH), np.arange(PATCH)
    angle = turn * (np.outer(freq, place) % PATCH)
    high, low = high_low(np.concatenate([np.cos(angle), -np.sin(angle)]))
    middle = np.tile((-1.0) ** place, (NYQ, 1)).astype(jnp.bfloat16)
    nothing = np.zeros_like(high)
    rows = np.concatenate(
        [np.concatenate([high, high], 1), np.concatenate([middle, middle], 1), np.concatenate([low, nothing], 1)]
    )
    angle = turn * (np.outer(place, full) % PATCH)
    cos, sin = np.cos(angle), np.sin(angle)
    high, low = high_low(np.block([[cos, -sin], [sin, cos]]))
    cols = np.concatenate([high, high, low])
    lags = np.arange(CROP) - CROP // 2
    ordered = np.concatenate([lags[0::2], lags[1::2]])
    weight = np.where(freq == 0, 1.0, 2.0) / PATCH**3
    angle = turn * (np.outer(ordered, freq) % PATCH)
    cos, sin = np.cos(angle) * weight, np.sin(angle) * weight
    high, low = high_low(np.block([[cos, -sin], [sin, cos]]))
    nothing = np.zeros_like(high)
    back_rows = np.block([[high, high], [low, nothing]])
    angle = turn * (np.outer(full, lags) % PATCH)
    one = np.concatenate([np.cos(angle), -np.sin(angle)])
    blank = np.zeros_like(one)
    high, low = high_low(np.block([[one, blank], [blank, one]]))
    back_cols = np.concatenate([high, low], 1)
    return rows, cols, back_rows, back_cols


def dot(left, right):
    return jnp.dot(left, right, preferred_element_type=F32)


def split(value):
    high = value.astype(BF16)
    return high, (value - high.astype(F32)).astype(BF16)


def patch_rows(mine, other, lower):
    edge = MARGIN
    zero = jnp.zeros((edge, mine.shape[1]), F32)
    a0, am, a3 = mine[:edge], mine[edge:-edge], mine[-edge:]
    o0, om, o3 = other[:edge], other[edge:-edge], other[-edge:]
    b0, b3 = jnp.where(lower, a0, o0), jnp.where(lower, o3, a3)
    n0, n3 = jnp.where(lower, zero, a0), jnp.where(lower, a3, zero)
    return [jnp.concatenate(x) for x in ((n0, am, n3), (b0, am, b3), (b0, om, b3))]


def spectrum(pixels, rows, cols, left):
    tiles = pixels.shape[1] // LANES
    patches = pixels.shape[1] // STRIDE
    found = dot(rows, jnp.concatenate(split(pixels)))
    parts = split(found[:PATCH] + found[PATCH + NYQ :])
    middle = found[PATCH : PATCH + 8]
    lane = lax.broadcasted_iota(jnp.int32, (PATCH, LANES), 1)

    def pick(value, j):
        tile = j // 2
        here = value[:, tile * LANES : (tile + 1) * LANES]
        beside = tile + 1 if j % 2 else tile - 1
        if 0 <= beside < tiles:
            there = value[:, beside * LANES : (beside + 1) * LANES]
        else:
            there = jnp.zeros_like(here)
        at = lane[: value.shape[0]]
        return jnp.where(at >= MARGIN if j % 2 else at < LANES - MARGIN, here, there)

    width = 2 * PATCH
    for j in range(patches):
        at = slice(j * HALF, (j + 1) * HALF)
        for base, value in zip((0, width), parts):
            own = pick(value, j)
            left[at, base : base + PATCH] = own[:HALF]
            left[at, base + PATCH : base + width] = own[HALF:]
            if base == 0:
                left[at, 2 * width : 2 * width + PATCH] = own[:HALF]
                left[at, 2 * width + PATCH :] = own[HALF:]
    line = lax.broadcasted_iota(jnp.int32, (8, LANES), 0)
    gathered = jnp.zeros((8, LANES), F32)
    for j in range(patches):
        gathered = jnp.where(line == j, pick(middle, j), gathered)
    high, low = split(jnp.concatenate([gathered, jnp.zeros_like(gathered)]))
    at = slice(patches * HALF, patches * HALF + NYQ)
    blank = jnp.zeros((NYQ, PATCH), BF16)
    for base, value in zip((0, width, 2 * width), (high, low, high)):
        left[at, base : base + PATCH] = value
        left[at, base + PATCH : base + width] = blank
    return dot(left[...], cols[...])


def surface(own, back, back_rows, back_cols, right, lagged):
    patches = (own.shape[0] - NYQ) // HALF
    xr, xi = own[:, :PATCH], own[:, PATCH:]
    yr, yi = back[:, :PATCH], back[:, PATCH:]
    zr, zi = xr * yr + xi * yi, xi * yr - xr * yi
    for j in range(patches):
        at, lanes = slice(j * HALF, (j + 1) * HALF), slice(j * LANES, (j + 1) * LANES)
        for base, value in zip((0, HALF), (zr, zi)):
            high, low = split(value[at])
            right[base : base + HALF, lanes] = high
            right[PATCH + base : PATCH + base + HALF, lanes] = low
    found = dot(back_rows[...], right[...])
    found = found[:PATCH] + found[PATCH:]
    for part in range(2):
        for parity in range(2):
            start = part * CROP + parity * PAIRS
            for j in range(patches):
                block = found[start : start + PAIRS, j * LANES : (j + 1) * LANES]
                lagged[2 * parity + part, pl.ds(j, PAIRS, stride=patches), :] = block
    at = slice(patches * HALF, patches * HALF + patches)
    mr, mi = zr[at] * (1.0 / PATCH**3), zi[at] * (1.0 / PATCH**3)
    value = []
    for q, mid in enumerate((mr, mi, -mr, -mi)):
        plane = lagged[q].reshape(PAIRS, patches, LANES) + mid[None]
        value.append(plane.reshape(PAIRS * patches, LANES))
    value = jnp.concatenate(value, 1)
    found = dot(jnp.concatenate(split(value)), back_cols[...])
    found = found[: PAIRS * patches] + found[PAIRS * patches :]
    return found[:, :LANES] + found[:, LANES:]


def own_kernel(mine, other, rows, cols, out, left):
    lower = lax.axis_index("pln") == 1
    for r, pixels in enumerate(patch_rows(mine[...], other[...], lower)):
        out[r] = spectrum(pixels, rows[...], cols, left.at[r])


def first_kernel(mine, other, own, rows, cols, back_rows, back_cols, out, left, right, lagged):
    lower = lax.axis_index("pln") == 1
    for r, pixels in enumerate(patch_rows(mine[...], other[...], lower)):
        back = spectrum(pixels, rows[...], cols, left.at[r])
        out[r] = surface(own[r], back, back_rows, back_cols, right.at[r], lagged.at[r])


def second_kernel(mine, other, own, first, rows, cols, back_rows, back_cols, out, left, right, lagged):
    pln = lax.axis_index("pln")
    lower = pln == 1
    patches = out.shape[1]
    line = lax.broadcasted_iota(jnp.int32, (PAIRS, patches, LANES), 1)
    mixed = []
    for r, pixels in enumerate(patch_rows(mine[...], other[...], lower)):
        back = spectrum(pixels, rows[...], cols, left.at[r])
        two = surface(own[r], back, back_rows, back_cols, right.at[r], lagged.at[r])
        one = first[r]
        joined = (one + two + one * two).reshape(PAIRS, patches, LANES)
        before = jnp.where(line == 0, 0.0, pltpu.roll(joined, 1, 1))
        after = jnp.where(line == patches - 1, 0.0, pltpu.roll(joined, patches - 1, 1))
        mixed.append((2.0 * joined + before + after) * (1.0 / 16.0))
    outer = 2.0 * mixed[0] + mixed[1]
    inner = mixed[0] + 2.0 * mixed[1] + mixed[2]
    for pair in range(PAIRS):
        lanes = slice(pair * LANES, (pair + 1) * LANES)
        out[pln, :, lanes] = outer[pair]
        out[1 - pln, :, lanes] = inner[pair]


def from_sections(tile, distance, ring):
    count = lax.axis_size("sec")
    route = [(i, (i + distance) % count) for i in range(count) if ring or i + distance < count]
    return lax.ppermute(tile, "sec", route)


def sibling(tile):
    return lax.ppermute(tile, "pln", [(0, 1), (1, 0)])


def body(section_tiles):
    tile = section_tiles[0]
    height, width = tile.shape
    patches = width // STRIDE
    assert height == PATCH and lax.axis_size("pln") == 2 and patches == 8
    rows, cols, back_rows, back_cols = tables()
    packed = patches * HALF + NYQ
    spread = 3
    left = pltpu.VMEM((spread, packed, 6 * PATCH), BF16)
    right = pltpu.VMEM((spread, 2 * PATCH, patches * LANES), BF16)
    lagged = pltpu.VMEM((spread, 4, PAIRS * patches, LANES), F32)
    params = pltpu.CompilerParams(vmem_limit_bytes=48 * 2**20)

    one_back = from_sections(tile, 1, False)
    two_back = from_sections(tile, 2, False)
    own = pl.pallas_call(
        own_kernel,
        out_shape=jax.ShapeDtypeStruct((spread, packed, 2 * PATCH), F32),
        scratch_shapes=[left],
        compiler_params=params,
    )(tile, sibling(tile), rows, cols)
    first = pl.pallas_call(
        first_kernel,
        out_shape=jax.ShapeDtypeStruct((spread, PAIRS * patches, LANES), F32),
        scratch_shapes=[left, right, lagged],
        compiler_params=params,
    )(one_back, sibling(one_back), own, rows, cols, back_rows, back_cols)
    mixed = pl.pallas_call(
        second_kernel,
        out_shape=jax.ShapeDtypeStruct((2, patches, CROP * CROP), F32),
        scratch_shapes=[left, right, lagged],
        compiler_params=params,
    )(two_back, sibling(two_back), own, first, rows, cols, back_rows, back_cols)
    return mixed[None]


def solution(mesh):
    placed = (P(("blocks", "sec"), "pln", None),)
    return jax.shard_map(
        body,
        mesh=mesh,
        in_specs=placed,
        out_specs=P(("blocks", "sec"), "pln", None, None),
        check_vma=False,
    )
```

```python
import functools

import jax
import jax.numpy as jnp
import numpy as np
from jax import lax
from jax.experimental import pallas as pl
from jax.experimental.pallas import tpu as pltpu
from jax.sharding import PartitionSpec as P

PATCH = 128
STRIDE = 64
CROP = 64
MARGIN = 32
HALF = PATCH // 2
LANES = 128
PAIRS = CROP // 2
NYQ = 16

BF16 = jnp.bfloat16
F32 = jnp.float32


def high_low(table):
    table = np.asarray(table, np.float32)
    high = table.astype(jnp.bfloat16)
    low = (table - high.astype(np.float32)).astype(jnp.bfloat16)
    return high, low


def tables():
    turn = 2.0 * np.pi / PATCH
    freq, place, full = np.arange(HALF), np.arange(PATCH), np.arange(PATCH)
    angle = turn * (np.outer(freq, place) % PATCH)
    high, low = high_low(np.concatenate([np.cos(angle), -np.sin(angle)]))
    middle = np.tile((-1.0) ** place, (NYQ, 1)).astype(jnp.bfloat16)
    nothing = np.zeros_like(high)
    rows = np.concatenate(
        [np.concatenate([high, high], 1), np.concatenate([middle, middle], 1), np.concatenate([low, nothing], 1)]
    )
    angle = turn * (np.outer(place, full) % PATCH)
    cos, sin = np.cos(angle), np.sin(angle)
    high, low = high_low(np.block([[cos, -sin], [sin, cos]]))
    cols = np.concatenate([high, high, low])
    lags = np.arange(CROP) - CROP // 2
    angle = turn * (np.outer(full, lags) % PATCH)
    cos, sin = np.cos(angle), np.sin(angle)
    high, low = high_low(np.block([[cos, sin], [-sin, cos]]))
    back_cols = np.concatenate([high, low], 1)
    ordered = np.concatenate([lags[0::2], lags[1::2]])
    weight = np.where(freq == 0, 1.0, 2.0) / PATCH**3
    angle = turn * (np.outer(ordered, freq) % PATCH)
    high, low = high_low(np.concatenate([np.cos(angle) * weight, -np.sin(angle) * weight]))
    back_rows = np.concatenate([high, high, low], 1)
    return rows, cols, back_rows, back_cols


def dot(left, right):
    return jnp.dot(left, right, preferred_element_type=F32)


def split(value):
    high = value.astype(BF16)
    return high, (value - high.astype(F32)).astype(BF16)


def outer_row(mine, lower):
    zero = jnp.zeros((MARGIN, mine.shape[1]), F32)
    first, last = mine[:MARGIN], mine[-MARGIN:]
    return jnp.concatenate([jnp.where(lower, zero, first), mine[MARGIN:-MARGIN], jnp.where(lower, last, zero)])


def inner_rows(mine, other, lower):
    first = jnp.where(lower, mine[:MARGIN], other[:MARGIN])
    last = jnp.where(lower, other[-MARGIN:], mine[-MARGIN:])
    return [jnp.concatenate([first, x[MARGIN:-MARGIN], last]) for x in (mine, other)]


def spectrum(pixels, rows, cols, left):
    tiles = pixels.shape[1] // LANES
    patches = pixels.shape[1] // STRIDE
    found = dot(rows, jnp.concatenate(split(pixels)))
    parts = split(found[:PATCH] + found[PATCH + NYQ :])
    middle = found[PATCH : PATCH + 8]
    lane = lax.broadcasted_iota(jnp.int32, (PATCH, LANES), 1)

    def pick(value, j):
        tile = j // 2
        here = value[:, tile * LANES : (tile + 1) * LANES]
        beside = tile + 1 if j % 2 else tile - 1
        if 0 <= beside < tiles:
            there = value[:, beside * LANES : (beside + 1) * LANES]
        else:
            there = jnp.zeros_like(here)
        at = lane[: value.shape[0]]
        return jnp.where(at >= MARGIN if j % 2 else at < LANES - MARGIN, here, there)

    width = 2 * PATCH
    for j in range(patches):
        at = slice(j * HALF, (j + 1) * HALF)
        for base, value in zip((0, width), parts):
            own = pick(value, j)
            left[at, base : base + PATCH] = own[:HALF]
            left[at, base + PATCH : base + width] = own[HALF:]
            if base == 0:
                left[at, 2 * width : 2 * width + PATCH] = own[:HALF]
                left[at, 2 * width + PATCH :] = own[HALF:]
    line = lax.broadcasted_iota(jnp.int32, (8, LANES), 0)
    gathered = jnp.zeros((8, LANES), F32)
    for j in range(patches):
        gathered = jnp.where(line == j, pick(middle, j), gathered)
    high, low = split(jnp.concatenate([gathered, jnp.zeros_like(gathered)]))
    at = slice(patches * HALF, patches * HALF + NYQ)
    blank = jnp.zeros((NYQ, PATCH), BF16)
    for base, value in zip((0, width, 2 * width), (high, low, high)):
        left[at, base : base + PATCH] = value
        left[at, base + PATCH : base + width] = blank
    return dot(left[...], cols[...])


def surface(own, back, back_rows, back_cols, right, lagged):
    patches = (own.shape[0] - NYQ) // HALF
    xr, xi = own[:, :PATCH], own[:, PATCH:]
    yr, yi = back[:, :PATCH], back[:, PATCH:]
    product = jnp.concatenate([xr * yr + xi * yi, xi * yr - xr * yi], 1)
    found = dot(jnp.concatenate(split(product)), back_cols[...])
    size = own.shape[0]
    found = (found[:size, :LANES] + found[size:, :LANES]) + (found[:size, LANES:] + found[size:, LANES:])
    high, low = split(found[: patches * HALF])
    for j in range(patches):
        at, lanes = slice(j * HALF, (j + 1) * HALF), slice(j * LANES, (j + 1) * LANES)
        right[:HALF, lanes] = high[at]
        right[HALF : 2 * HALF, lanes] = low[at]
        right[2 * HALF :, lanes] = high[at]
    middle = found[patches * HALF : patches * HALF + patches] * (1.0 / PATCH**3)
    found = dot(back_rows[...], right[...])
    lane = lax.broadcasted_iota(jnp.int32, (PAIRS, LANES), 1)
    for j in range(patches):
        lanes = slice(j * LANES, (j + 1) * LANES)
        cos_even, cos_odd, sin_even, sin_odd = (found[q * PAIRS : (q + 1) * PAIRS, lanes] for q in range(4))
        stay = jnp.where(lane < CROP, cos_even, sin_odd)
        move = jnp.where(lane < CROP, cos_odd, sin_even)
        lagged[pl.ds(j, PAIRS, stride=patches), :] = stay + pltpu.roll(move, CROP, 1)
    middle = jnp.where(lane[:patches] < CROP, middle, -pltpu.roll(middle, CROP, 1))
    return lagged[...].reshape(PAIRS, patches, LANES) + middle[None]


def own_kernel(mine, other, rows, cols, out, left):
    lower = lax.axis_index("pln") == 1
    mine, other = mine[...], other[...]
    for r, pixels in enumerate([outer_row(mine, lower)] + inner_rows(mine, other, lower)):
        out[r] = spectrum(pixels, rows[...], cols, left.at[r])


def first_kernel(mine, other, own, rows, cols, back_rows, back_cols, out, left, right, lagged):
    lower = lax.axis_index("pln") == 1
    mine, other = mine[...], other[1 - lax.axis_index("pln")]
    for r, pixels in enumerate([outer_row(mine, lower)] + inner_rows(mine, other, lower)):
        back = spectrum(pixels, rows[...], cols, left.at[r])
        out[r] = surface(own[r], back, back_rows, back_cols, right.at[r], lagged.at[r])


def joined_row(one, two):
    joined = one + two + one * two
    patches = joined.shape[1]
    line = lax.broadcasted_iota(jnp.int32, joined.shape, 1)
    before = jnp.where(line == 0, 0.0, pltpu.roll(joined, 1, 1))
    after = jnp.where(line == patches - 1, 0.0, pltpu.roll(joined, patches - 1, 1))
    return (2.0 * joined + before + after) * (1.0 / 16.0)


def outer_kernel(mine, own, first, rows, cols, back_rows, back_cols, out, left, right, lagged):
    lower = lax.axis_index("pln") == 1
    back = spectrum(outer_row(mine[...], lower), rows[...], cols, left)
    out[...] = joined_row(first[0], surface(own[0], back, back_rows, back_cols, right, lagged))


def inner_kernel(mine, other, own, first, outer, rows, cols, back_rows, back_cols, out, left, right, lagged):
    pln = lax.axis_index("pln")
    mixed = []
    for r, pixels in enumerate(inner_rows(mine[...], other[...], pln == 1)):
        back = spectrum(pixels, rows[...], cols, left.at[r])
        two = surface(own[r + 1], back, back_rows, back_cols, right.at[r], lagged.at[r])
        mixed.append(joined_row(first[r + 1], two))
    ending = outer[...]
    ends = 2.0 * ending + mixed[0]
    inside = ending + 2.0 * mixed[0] + mixed[1]
    for pair in range(PAIRS):
        lanes = slice(pair * LANES, (pair + 1) * LANES)
        out[pln, :, lanes] = ends[pair]
        out[1 - pln, :, lanes] = inside[pair]


def from_sections(tile, distance, ring):
    count = lax.axis_size("sec")
    route = [(i, (i + distance) % count) for i in range(count) if ring or i + distance < count]
    return lax.ppermute(tile, "sec", route)


def sibling(tile):
    return lax.ppermute(tile, "pln", [(0, 1), (1, 0)])


def body(section_tiles):
    tile = section_tiles[0]
    height, width = tile.shape
    patches = width // STRIDE
    assert height == PATCH and lax.axis_size("pln") == 2 and patches == 8
    rows, cols, back_rows, back_cols = tables()
    packed = patches * HALF + NYQ
    surfaces = (PAIRS, patches, LANES)

    def call(kernel, shape, spread, micros, *args):
        scratch = [
            pltpu.VMEM(spread + (packed, 6 * PATCH), BF16),
            pltpu.VMEM(spread + (3 * HALF, patches * LANES), BF16),
            pltpu.VMEM(spread + (PAIRS * patches, LANES), F32),
        ]
        return pl.pallas_call(
            kernel,
            out_shape=jax.ShapeDtypeStruct(shape, F32),
            scratch_shapes=scratch[:1] if kernel is own_kernel else scratch,
            cost_estimate=pl.CostEstimate(flops=int(micros * 1e7), bytes_accessed=int(micros * 3e4), transcendentals=0),
            compiler_params=pltpu.CompilerParams(vmem_limit_bytes=48 * 2**20),
        )(*args)

    one_back = from_sections(tile, 1, False)
    two_back = from_sections(tile, 2, False)
    own = call(own_kernel, (3, packed, 2 * PATCH), (3,), 1.4, tile, sibling(tile), rows, cols)
    one_back, own = lax.optimization_barrier((one_back, own))
    first = call(first_kernel, (3,) + surfaces, (3,), 3.6, one_back, lax.all_gather(one_back, 'pln'), own, rows, cols, back_rows, back_cols)
    two_back, first = lax.optimization_barrier((two_back, first))
    other = sibling(two_back)
    outer = call(outer_kernel, surfaces, (), 1.5, two_back, own, first, rows, cols, back_rows, back_cols)
    mixed = call(
        inner_kernel, (2, patches, CROP * CROP), (2,), 3.0, two_back, other, own, first, outer, rows, cols, back_rows, back_cols
    )
    return mixed[None]


def solution(mesh):
    placed = (P(("blocks", "sec"), "pln", None),)
    return jax.shard_map(
        body,
        mesh=mesh,
        in_specs=placed,
        out_specs=P(("blocks", "sec"), "pln", None, None),
        check_vma=False,
    )
```

```python
import functools

import jax
import jax.numpy as jnp
import numpy as np
from jax import lax
from jax.experimental import pallas as pl
from jax.experimental.pallas import tpu as pltpu
from jax.sharding import PartitionSpec as P

PATCH = 128
STRIDE = 64
CROP = 64
MARGIN = 32
HALF = PATCH // 2
LANES = 128
PAIRS = CROP // 2
NYQ = 16

BF16 = jnp.bfloat16
F32 = jnp.float32


def high_low(table):
    table = np.asarray(table, np.float32)
    high = table.astype(jnp.bfloat16)
    low = (table - high.astype(np.float32)).astype(jnp.bfloat16)
    return high, low


def tables():
    turn = 2.0 * np.pi / PATCH
    freq, place, full = np.arange(HALF), np.arange(PATCH), np.arange(PATCH)
    angle = turn * (np.outer(freq, place) % PATCH)
    high, low = high_low(np.concatenate([np.cos(angle), -np.sin(angle)]))
    middle = np.tile((-1.0) ** place, (NYQ, 1)).astype(jnp.bfloat16)
    nothing = np.zeros_like(high)
    rows = np.concatenate(
        [np.concatenate([high, high], 1), np.concatenate([middle, middle], 1), np.concatenate([low, nothing], 1)]
    )
    angle = turn * (np.outer(place, full) % PATCH)
    cos, sin = np.cos(angle), np.sin(angle)
    high, low = high_low(np.block([[cos, -sin], [sin, cos]]))
    cols = np.concatenate([high, high, low])
    lags = np.arange(CROP) - CROP // 2
    angle = turn * (np.outer(full, lags) % PATCH)
    cos, sin = np.cos(angle), np.sin(angle)
    high, low = high_low(np.block([[cos, sin], [-sin, cos]]))
    back_cols = np.concatenate([high, low], 1)
    ordered = np.concatenate([lags[0::2], lags[1::2]])
    weight = np.where(freq == 0, 1.0, 2.0) / PATCH**3
    angle = turn * (np.outer(ordered, freq) % PATCH)
    high, low = high_low(np.concatenate([np.cos(angle) * weight, -np.sin(angle) * weight]))
    back_rows = np.concatenate([high, high, low, low], 1)
    parts = (rows, cols, back_rows, back_cols)
    ends = np.cumsum([len(x) for x in parts])
    return np.concatenate(parts), [slice(int(end) - len(x), int(end)) for x, end in zip(parts, ends)]


def dot(left, right):
    return jnp.dot(left, right, preferred_element_type=F32)


def split(value):
    high = value.astype(BF16)
    return high, (value - high.astype(F32)).astype(BF16)


def outer_row(mine, lower):
    zero = jnp.zeros((MARGIN, mine.shape[1]), F32)
    first, last = mine[:MARGIN], mine[-MARGIN:]
    return jnp.concatenate([jnp.where(lower, zero, first), mine[MARGIN:-MARGIN], jnp.where(lower, last, zero)])


def inner_rows(mine, other, lower):
    first = jnp.where(lower, mine[:MARGIN], other[:MARGIN])
    last = jnp.where(lower, other[-MARGIN:], mine[-MARGIN:])
    return [jnp.concatenate([first, x[MARGIN:-MARGIN], last]) for x in (mine, other)]


def expand(pixels, rows, left):
    tiles = pixels.shape[1] // LANES
    patches = pixels.shape[1] // STRIDE
    found = dot(rows[...], jnp.concatenate(split(pixels)))
    parts = split(found[:PATCH] + found[PATCH + NYQ :])
    middle = found[PATCH : PATCH + 8]
    lane = lax.broadcasted_iota(jnp.int32, (PATCH, LANES), 1)

    def pick(value, j):
        tile = j // 2
        here = value[:, tile * LANES : (tile + 1) * LANES]
        beside = tile + 1 if j % 2 else tile - 1
        if 0 <= beside < tiles:
            there = value[:, beside * LANES : (beside + 1) * LANES]
        else:
            there = jnp.zeros_like(here)
        at = lane[: value.shape[0]]
        return jnp.where(at >= MARGIN if j % 2 else at < LANES - MARGIN, here, there)

    width = 2 * PATCH
    for j in range(patches):
        at = slice(j * HALF, (j + 1) * HALF)
        for base, value in zip((0, width), parts):
            own = pick(value, j)
            left[at, base : base + PATCH] = own[:HALF]
            left[at, base + PATCH : base + width] = own[HALF:]
            if base == 0:
                left[at, 2 * width : 2 * width + PATCH] = own[:HALF]
                left[at, 2 * width + PATCH :] = own[HALF:]
    line = lax.broadcasted_iota(jnp.int32, (8, LANES), 0)
    gathered = jnp.zeros((8, LANES), F32)
    for j in range(patches):
        gathered = jnp.where(line == j, pick(middle, j), gathered)
    high, low = split(jnp.concatenate([gathered, jnp.zeros_like(gathered)]))
    at = slice(patches * HALF, patches * HALF + NYQ)
    blank = jnp.zeros((NYQ, PATCH), BF16)
    for base, value in zip((0, width, 2 * width), (high, low, high)):
        left[at, base : base + PATCH] = value
        left[at, base + PATCH : base + width] = blank


def spectra(pixels, rows, cols, left, out):
    for r, x in enumerate(pixels):
        expand(x, rows, left.at[r])
    for r in range(len(pixels)):
        out[r] = dot(left[r], cols[...])


def multiply(own, back, back_cols, half):
    size = own.shape[0]
    xr, xi = own[:, :PATCH], own[:, PATCH:]
    yr, yi = back[:, :PATCH], back[:, PATCH:]
    product = jnp.concatenate([xr * yr + xi * yi, xi * yr - xr * yi], 1)
    found = dot(jnp.concatenate(split(product)), back_cols[...])
    half[...] = (found[:size, :LANES] + found[size:, :LANES]) + (found[:size, LANES:] + found[size:, LANES:])


def finish(half, back_rows, right, lagged):
    patches = (half.shape[0] - NYQ) // HALF
    high, low = split(half[: patches * HALF])
    for j in range(patches):
        at, lanes = slice(j * HALF, (j + 1) * HALF), slice(j * LANES, (j + 1) * LANES)
        right[:HALF, lanes] = high[at]
        right[HALF : 2 * HALF, lanes] = low[at]
        right[2 * HALF : 3 * HALF, lanes] = high[at]
        right[3 * HALF :, lanes] = low[at]
    middle = half[patches * HALF : patches * HALF + patches] * (1.0 / PATCH**3)
    found = dot(back_rows[...], right[...])
    lane = lax.broadcasted_iota(jnp.int32, (PAIRS, LANES), 1)
    for j in range(patches):
        lanes = slice(j * LANES, (j + 1) * LANES)
        cos_even, cos_odd, sin_even, sin_odd = (found[q * PAIRS : (q + 1) * PAIRS, lanes] for q in range(4))
        stay = jnp.where(lane < CROP, cos_even, sin_odd)
        move = jnp.where(lane < CROP, cos_odd, sin_even)
        lagged[pl.ds(j, PAIRS, stride=patches), :] = stay + pltpu.roll(move, CROP, 1)
    middle = jnp.where(lane[:patches] < CROP, middle, -pltpu.roll(middle, CROP, 1))
    return lagged[...].reshape(PAIRS, patches, LANES) + middle[None]


def surfaces(pixels, own, rows, cols, back_rows, back_cols, left, spec, half, right, lagged):
    spectra(pixels, rows, cols, left, spec)
    for r in range(len(pixels)):
        multiply(own(r), spec[r], back_cols, half.at[r])
    return lambda r: finish(half.at[r], back_rows, right.at[r], lagged.at[r])


def own_kernel(at, mine, other, table, out, left, *_):
    rows, cols = table.at[at[0]], table.at[at[1]]
    lower = lax.axis_index("pln") == 1
    mine, other = mine[...], other[...]
    spectra([outer_row(mine, lower)] + inner_rows(mine, other, lower), rows, cols, left, out)


def reached(distance, work):
    present = lax.axis_index("sec") >= distance
    pl.when(present)(lambda: work(True))
    pl.when(jnp.logical_not(present))(lambda: work(False))


def first_kernel(at, mine, both, own, table, out, *scratch):
    pln = lax.axis_index("pln")

    def work(present):
        if not present:
            out[...] = jnp.zeros_like(out)
            return
        here, there = mine[...], both[1 - pln]
        pixels = [outer_row(here, pln == 1)] + inner_rows(here, there, pln == 1)
        found = surfaces(pixels, lambda r: own[r], *(table.at[x] for x in at), *scratch)
        for r in range(len(pixels)):
            out[r] = found(r)

    reached(1, work)


def joined_row(one, two):
    joined = one + two + one * two
    patches = joined.shape[1]
    line = lax.broadcasted_iota(jnp.int32, joined.shape, 1)
    before = jnp.where(line == 0, 0.0, pltpu.roll(joined, 1, 1))
    after = jnp.where(line == patches - 1, 0.0, pltpu.roll(joined, patches - 1, 1))
    return (2.0 * joined + before + after) * (1.0 / 16.0)


def outer_kernel(at, mine, own, first, table, out, *scratch):
    def work(present):
        found = jnp.zeros_like
        if present:
            pixels = [outer_row(mine[...], lax.axis_index("pln") == 1)]
            got = surfaces(pixels, lambda r: own[r], *(table.at[x] for x in at), *scratch)
            found = lambda _: got(0)
        one = first[0]
        out[...] = joined_row(one, found(one))

    reached(2, work)


def inner_kernel(at, mine, other, own, first, outer, table, out, *scratch):
    pln = lax.axis_index("pln")

    def work(present):
        found = lambda r: jnp.zeros(outer.shape, F32)
        if present:
            pixels = inner_rows(mine[...], other[...], pln == 1)
            found = surfaces(pixels, lambda r: own[r + 1], *(table.at[x] for x in at), *scratch)
        near, far = (joined_row(first[r + 1], found(r)) for r in range(2))
        ending = outer[...]
        ends = 2.0 * ending + near
        inside = ending + 2.0 * near + far
        for pair in range(PAIRS):
            lanes = slice(pair * LANES, (pair + 1) * LANES)
            out[pln, :, lanes] = ends[pair]
            out[1 - pln, :, lanes] = inside[pair]

    reached(2, work)


def from_sections(tile, distance, ring):
    count = lax.axis_size("sec")
    route = [(i, (i + distance) % count) for i in range(count) if ring or i + distance < count]
    return lax.ppermute(tile, "sec", route)


def sibling(tile):
    return lax.ppermute(tile, "pln", [(0, 1), (1, 0)])


def body(section_tiles):
    tile = section_tiles[0]
    height, width = tile.shape
    patches = width // STRIDE
    assert height == PATCH and lax.axis_size("pln") == 2 and patches == 8
    table, at = tables()
    packed = patches * HALF + NYQ
    shape = (PAIRS, patches, LANES)

    def call(kernel, shape, spread, *args):
        scratch = [
            pltpu.VMEM((spread, packed, 6 * PATCH), BF16),
            pltpu.VMEM((spread, packed, 2 * PATCH), F32),
            pltpu.VMEM((spread, packed, LANES), F32),
            pltpu.VMEM((spread, 4 * HALF, patches * LANES), BF16),
            pltpu.VMEM((spread, PAIRS * patches, LANES), F32),
        ]
        return pl.pallas_call(
            functools.partial(kernel, at),
            out_shape=jax.ShapeDtypeStruct(shape, F32),
            scratch_shapes=scratch,
            compiler_params=pltpu.CompilerParams(vmem_limit_bytes=40 * 2**20),
        )(*args)

    one_back = from_sections(tile, 1, True)
    own = call(own_kernel, (3, packed, 2 * PATCH), 3, tile, sibling(tile), table)
    two_back = from_sections(tile, 2, True)
    one_back, own = lax.optimization_barrier((one_back, own))
    first = call(first_kernel, (3,) + shape, 3, one_back, lax.all_gather(one_back, "pln"), own, table)
    two_back, first = lax.optimization_barrier((two_back, first))
    other = sibling(two_back)
    outer = call(outer_kernel, shape, 1, two_back, own, first, table)
    mixed = call(inner_kernel, (2, patches, CROP * CROP), 2, two_back, other, own, first, outer, table)
    return mixed[None]


def solution(mesh):
    placed = (P(("blocks", "sec"), "pln", None),)
    return jax.shard_map(
        body,
        mesh=mesh,
        in_specs=placed,
        out_specs=P(("blocks", "sec"), "pln", None, None),
        check_vma=False,
    )
```

```python
import functools

import jax
import jax.numpy as jnp
import numpy as np
from jax import lax
from jax.experimental import pallas as pl
from jax.experimental.pallas import tpu as pltpu
from jax.sharding import PartitionSpec as P

PATCH = 128
STRIDE = 64
CROP = 64
MARGIN = 32
HALF = PATCH // 2
LANES = 128
PAIRS = CROP // 2
NYQ = 16

BF16 = jnp.bfloat16
F32 = jnp.float32


def high_low(table):
    table = np.asarray(table, np.float32)
    high = table.astype(jnp.bfloat16)
    low = (table - high.astype(np.float32)).astype(jnp.bfloat16)
    return high, low


def tables():
    turn = 2.0 * np.pi / PATCH
    freq, place, full = np.arange(HALF), np.arange(PATCH), np.arange(PATCH)
    angle = turn * (np.outer(freq, place) % PATCH)
    high, low = high_low(np.concatenate([np.cos(angle), -np.sin(angle)]))
    middle = np.tile((-1.0) ** place, (NYQ, 1)).astype(jnp.bfloat16)
    nothing = np.zeros_like(high)
    rows = np.concatenate(
        [np.concatenate([high, high], 1), np.concatenate([middle, middle], 1), np.concatenate([low, nothing], 1)]
    )
    angle = turn * (np.outer(place, full) % PATCH)
    cos, sin = np.cos(angle), np.sin(angle)
    high, low = high_low(np.block([[cos, -sin], [sin, cos]]))
    cols = np.concatenate([high, high, low])
    lags = np.arange(CROP) - CROP // 2
    angle = turn * (np.outer(full, lags) % PATCH)
    cos, sin = np.cos(angle), np.sin(angle)
    high, low = high_low(np.block([[cos, sin], [-sin, cos]]))
    back_cols = np.concatenate([high, low], 1)
    ordered = np.concatenate([lags[0::2], lags[1::2]])
    weight = np.where(freq == 0, 1.0, 2.0) / PATCH**3
    angle = turn * (np.outer(ordered, freq) % PATCH)
    high, low = high_low(np.concatenate([np.cos(angle) * weight, -np.sin(angle) * weight]))
    back_rows = np.concatenate([high, high, low, low], 1)
    parts = (rows, cols, back_rows, back_cols)
    ends = np.cumsum([len(x) for x in parts])
    return np.concatenate(parts), [slice(int(end) - len(x), int(end)) for x, end in zip(parts, ends)]


def dot(left, right):
    return jnp.dot(left, right, preferred_element_type=F32)


def split(value):
    high = value.astype(BF16)
    return high, (value - high.astype(F32)).astype(BF16)


def outer_row(mine, lower):
    zero = jnp.zeros((MARGIN, mine.shape[1]), F32)
    first, last = mine[:MARGIN], mine[-MARGIN:]
    return jnp.concatenate([jnp.where(lower, zero, first), mine[MARGIN:-MARGIN], jnp.where(lower, last, zero)])


def inner_rows(mine, other, lower):
    first = jnp.where(lower, mine[:MARGIN], other[:MARGIN])
    last = jnp.where(lower, other[-MARGIN:], mine[-MARGIN:])
    return [jnp.concatenate([first, x[MARGIN:-MARGIN], last]) for x in (mine, other)]


def expand(pixels, rows, left):
    tiles = pixels.shape[1] // LANES
    patches = pixels.shape[1] // STRIDE
    found = dot(rows[...], jnp.concatenate(split(pixels)))
    parts = split(found[:PATCH] + found[PATCH + NYQ :])
    middle = found[PATCH : PATCH + 8]
    lane = lax.broadcasted_iota(jnp.int32, (PATCH, LANES), 1)

    def pick(value, j):
        tile = j // 2
        here = value[:, tile * LANES : (tile + 1) * LANES]
        beside = tile + 1 if j % 2 else tile - 1
        if 0 <= beside < tiles:
            there = value[:, beside * LANES : (beside + 1) * LANES]
        else:
            there = jnp.zeros_like(here)
        at = lane[: value.shape[0]]
        return jnp.where(at >= MARGIN if j % 2 else at < LANES - MARGIN, here, there)

    width = 2 * PATCH
    for j in range(patches):
        at = slice(j * HALF, (j + 1) * HALF)
        for base, value in zip((0, width), parts):
            own = pick(value, j)
            left[at, base : base + PATCH] = own[:HALF]
            left[at, base + PATCH : base + width] = own[HALF:]
            if base == 0:
                left[at, 2 * width : 2 * width + PATCH] = own[:HALF]
                left[at, 2 * width + PATCH :] = own[HALF:]
    line = lax.broadcasted_iota(jnp.int32, (8, LANES), 0)
    gathered = jnp.zeros((8, LANES), F32)
    for j in range(patches):
        gathered = jnp.where(line == j, pick(middle, j), gathered)
    high, low = split(jnp.concatenate([gathered, jnp.zeros_like(gathered)]))
    at = slice(patches * HALF, patches * HALF + NYQ)
    blank = jnp.zeros((NYQ, PATCH), BF16)
    for base, value in zip((0, width, 2 * width), (high, low, high)):
        left[at, base : base + PATCH] = value
        left[at, base + PATCH : base + width] = blank


def spectra(pixels, rows, cols, left, out):
    for r, x in enumerate(pixels):
        expand(x, rows, left.at[r])
    for r in range(len(pixels)):
        out[r] = dot(left[r], cols[...])


def multiply(own, back, back_cols, half):
    size = own.shape[0]
    xr, xi = own[:, :PATCH], own[:, PATCH:]
    yr, yi = back[:, :PATCH], back[:, PATCH:]
    product = jnp.concatenate([xr * yr + xi * yi, xi * yr - xr * yi], 1)
    found = dot(jnp.concatenate(split(product)), back_cols[...])
    half[...] = (found[:size, :LANES] + found[size:, :LANES]) + (found[:size, LANES:] + found[size:, LANES:])


def stack(half, right):
    patches = (half.shape[0] - NYQ) // HALF
    high, low = split(half[: patches * HALF])
    for j in range(patches):
        at, lanes = slice(j * HALF, (j + 1) * HALF), slice(j * LANES, (j + 1) * LANES)
        for q, value in enumerate((high, low, high, low)):
            right[q * HALF : (q + 1) * HALF, lanes] = value[at]


def finish(half, back_rows, right, lagged):
    patches = (half.shape[0] - NYQ) // HALF
    middle = half[patches * HALF : patches * HALF + patches] * (1.0 / PATCH**3)
    found = dot(back_rows[...], right[...])
    lane = lax.broadcasted_iota(jnp.int32, (PAIRS, LANES), 1)
    for j in range(patches):
        lanes = slice(j * LANES, (j + 1) * LANES)
        cos_even, cos_odd, sin_even, sin_odd = (found[q * PAIRS : (q + 1) * PAIRS, lanes] for q in range(4))
        stay = jnp.where(lane < CROP, cos_even, sin_odd)
        move = jnp.where(lane < CROP, cos_odd, sin_even)
        lagged[pl.ds(j, PAIRS, stride=patches), :] = stay + pltpu.roll(move, CROP, 1)
    middle = jnp.where(lane[:patches] < CROP, middle, -pltpu.roll(middle, CROP, 1))
    return lagged[...].reshape(PAIRS, patches, LANES) + middle[None]


def surfaces(pixels, own, rows, cols, back_rows, back_cols, left, spec, half, right, lagged):
    spectra(pixels, rows, cols, left, spec)
    for r in range(len(pixels)):
        multiply(own(r), spec[r], back_cols, half.at[r])
    for r in range(len(pixels)):
        stack(half.at[r], right.at[r])
    return lambda r: finish(half.at[r], back_rows, right.at[r], lagged.at[r])


def own_kernel(at, mine, other, table, out, left, *_):
    rows, cols = table.at[at[0]], table.at[at[1]]
    lower = lax.axis_index("pln") == 1
    mine, other = mine[...], other[1 - lax.axis_index("pln")]
    spectra([outer_row(mine, lower)] + inner_rows(mine, other, lower), rows, cols, left, out)


def reached(distance, work):
    present = lax.axis_index("sec") >= distance
    pl.when(present)(lambda: work(True))
    pl.when(jnp.logical_not(present))(lambda: work(False))


def first_kernel(at, mine, both, own, table, out, *scratch):
    pln = lax.axis_index("pln")

    def work(present):
        if not present:
            out[...] = jnp.zeros_like(out)
            return
        here, there = mine[...], both[1 - pln]
        pixels = [outer_row(here, pln == 1)] + inner_rows(here, there, pln == 1)[:1]
        found = surfaces(pixels, lambda r: own[r], *(table.at[x] for x in at), *scratch)
        for r in range(len(pixels)):
            out[r] = found(r)

    reached(1, work)


def joined_row(one, two):
    joined = one + two + one * two
    patches = joined.shape[1]
    line = lax.broadcasted_iota(jnp.int32, joined.shape, 1)
    before = jnp.where(line == 0, 0.0, pltpu.roll(joined, 1, 1))
    after = jnp.where(line == patches - 1, 0.0, pltpu.roll(joined, patches - 1, 1))
    return (2.0 * joined + before + after) * (1.0 / 16.0)


def outer_kernel(at, mine, earlier, both, own, first, table, out, far, *scratch):
    pln, sec = lax.axis_index("pln"), lax.axis_index("sec")

    def work(present):
        parts = [table.at[x] for x in at]
        beyond = inner_rows(earlier[...], both[1 - pln], pln == 1)[1]
        one = first[0]
        if present:
            got = surfaces([outer_row(mine[...], pln == 1), beyond], lambda r: own[2 * r], *parts, *scratch)
            out[...] = joined_row(one, got(0))
            far[...] = got(1)
        else:
            got = surfaces([beyond], lambda r: own[2], *parts, *scratch)
            out[...] = joined_row(one, jnp.zeros_like(one))
            far[...] = jnp.where(sec >= 1, got(0), 0.0)

    reached(2, work)


def inner_kernel(at, mine, other, own, first, outer, beyond, table, out, left, spec, half, right, lagged, staged, sent):
    pln = lax.axis_index("pln")

    def send(slot, row, value):
        for pair in range(PAIRS):
            staged[slot, :, pair * LANES : (pair + 1) * LANES] = value[pair]
        copy = pltpu.make_async_copy(staged.at[slot], out.at[row], sent.at[slot])
        copy.start()
        return copy

    def work(present):
        found = lambda r: jnp.zeros(outer.shape, F32)
        if present:
            pixels = inner_rows(mine[...], other[...], pln == 1)
            parts = (table.at[x] for x in at)
            found = surfaces(pixels, lambda r: own[r + 1], *parts, left, spec, half, right, lagged)
        near = joined_row(first[1], found(0))
        ending = outer[...]
        copies = [send(0, pln, 2.0 * ending + near)]
        far = joined_row(beyond[...], found(1))
        copies.append(send(1, 1 - pln, ending + 2.0 * near + far))
        for copy in copies:
            copy.wait()

    reached(2, work)


def from_sections(tile, distance, ring):
    count = lax.axis_size("sec")
    route = [(i, (i + distance) % count) for i in range(count) if ring or i + distance < count]
    return lax.ppermute(tile, "sec", route)


def sibling(tile):
    return lax.ppermute(tile, "pln", [(0, 1), (1, 0)])


def body(section_tiles):
    tile = section_tiles[0]
    height, width = tile.shape
    patches = width // STRIDE
    assert height == PATCH and lax.axis_size("pln") == 2 and patches == 8
    table, at = tables()
    packed = patches * HALF + NYQ
    shape = (PAIRS, patches, LANES)

    def call(kernel, shape, spread, *args, outs=1):
        scratch = [
            pltpu.VMEM((spread, packed, 6 * PATCH), BF16),
            pltpu.VMEM((spread, packed, 2 * PATCH), F32),
            pltpu.VMEM((spread, packed, LANES), F32),
            pltpu.VMEM((spread, 4 * HALF, patches * LANES), BF16),
            pltpu.VMEM((spread, PAIRS * patches, LANES), F32),
        ]
        ending = [pltpu.VMEM(shape, F32), pltpu.SemaphoreType.DMA((2,))] if kernel is inner_kernel else []
        return pl.pallas_call(
            functools.partial(kernel, at),
            out_shape=[jax.ShapeDtypeStruct(shape, F32)] * outs,
            out_specs=[pl.BlockSpec(memory_space=pl.ANY if ending else pltpu.VMEM)] * outs,
            scratch_shapes=scratch + ending,
            compiler_params=pltpu.CompilerParams(vmem_limit_bytes=40 * 2**20),
        )(*args)

    one_back = from_sections(tile, 1, True)
    two_back = from_sections(tile, 2, True)
    (own,) = call(own_kernel, (3, packed, 2 * PATCH), 3, tile, lax.all_gather(tile, "pln"), table)
    one_back, own = lax.optimization_barrier((one_back, own))
    both = lax.all_gather(one_back, "pln")
    (first,) = call(first_kernel, (2,) + shape, 2, one_back, both, own, table)
    two_back, first = lax.optimization_barrier((two_back, first))
    other = sibling(two_back)
    outer, beyond = call(outer_kernel, shape, 2, two_back, one_back, both, own, first, table, outs=2)
    (mixed,) = call(inner_kernel, (2, patches, CROP * CROP), 2, two_back, other, own, first, outer, beyond, table)
    return mixed[None]


def solution(mesh):
    placed = (P(("blocks", "sec"), "pln", None),)
    return jax.shard_map(
        body,
        mesh=mesh,
        in_specs=placed,
        out_specs=P(("blocks", "sec"), "pln", None, None),
        check_vma=False,
    )
```

```python
import functools

import jax
import jax.numpy as jnp
import numpy as np
from jax import lax
from jax.experimental import pallas as pl
from jax.experimental.pallas import tpu as pltpu
from jax.sharding import PartitionSpec as P

PATCH = 128
STRIDE = 64
CROP = 64
MARGIN = 32
HALF = PATCH // 2
LANES = 128
PAIRS = CROP // 2
NYQ = 16

BF16 = jnp.bfloat16
F32 = jnp.float32


def high_low(table):
    table = np.asarray(table, np.float32)
    high = table.astype(jnp.bfloat16)
    low = (table - high.astype(np.float32)).astype(jnp.bfloat16)
    return high, low


def tables():
    turn = 2.0 * np.pi / PATCH
    freq, place, full = np.arange(HALF), np.arange(PATCH), np.arange(PATCH)
    angle = turn * (np.outer(freq, place) % PATCH)
    high, low = high_low(np.concatenate([np.cos(angle), -np.sin(angle)]))
    middle = np.tile((-1.0) ** place, (NYQ, 1)).astype(jnp.bfloat16)
    nothing = np.zeros_like(high)
    rows = np.concatenate(
        [np.concatenate([high, high], 1), np.concatenate([middle, middle], 1), np.concatenate([low, nothing], 1)]
    )
    angle = turn * (np.outer(place, full) % PATCH)
    cos, sin = np.cos(angle), np.sin(angle)
    high, low = high_low(np.block([[cos, -sin], [sin, cos]]))
    cols = np.concatenate([high, high, low])
    lags = np.arange(CROP) - CROP // 2
    angle = turn * (np.outer(full, lags) % PATCH)
    cos, sin = np.cos(angle), np.sin(angle)
    high, low = high_low(np.block([[cos, sin], [-sin, cos]]))
    back_cols = np.concatenate([high, low], 1)
    ordered = np.concatenate([lags[0::2], lags[1::2]])
    weight = np.where(freq == 0, 1.0, 2.0) / PATCH**3
    angle = turn * (np.outer(ordered, freq) % PATCH)
    high, low = high_low(np.concatenate([np.cos(angle) * weight, -np.sin(angle) * weight]))
    back_rows = np.concatenate([high, high, low, low], 1)
    parts = (rows, cols, back_rows, back_cols)
    ends = np.cumsum([len(x) for x in parts])
    return np.concatenate(parts), [slice(int(end) - len(x), int(end)) for x, end in zip(parts, ends)]


def dot(left, right):
    return jnp.dot(left, right, preferred_element_type=F32)


def split(value):
    high = value.astype(BF16)
    return high, (value - high.astype(F32)).astype(BF16)


def outer_row(mine, lower):
    zero = jnp.zeros((MARGIN, mine.shape[1]), F32)
    first, last = mine[:MARGIN], mine[-MARGIN:]
    return jnp.concatenate([jnp.where(lower, zero, first), mine[MARGIN:-MARGIN], jnp.where(lower, last, zero)])


def inner_rows(mine, other, lower):
    first = jnp.where(lower, mine[:MARGIN], other[:MARGIN])
    last = jnp.where(lower, other[-MARGIN:], mine[-MARGIN:])
    return [jnp.concatenate([first, x[MARGIN:-MARGIN], last]) for x in (mine, other)]


def expand(pixels, rows, left):
    tiles = pixels.shape[1] // LANES
    patches = pixels.shape[1] // STRIDE
    found = dot(rows[...], jnp.concatenate(split(pixels)))
    parts = split(found[:PATCH] + found[PATCH + NYQ :])
    middle = found[PATCH : PATCH + 8]
    lane = lax.broadcasted_iota(jnp.int32, (PATCH, LANES), 1)

    def pick(value, j):
        tile = j // 2
        here = value[:, tile * LANES : (tile + 1) * LANES]
        beside = tile + 1 if j % 2 else tile - 1
        if 0 <= beside < tiles:
            there = value[:, beside * LANES : (beside + 1) * LANES]
        else:
            there = jnp.zeros_like(here)
        at = lane[: value.shape[0]]
        return jnp.where(at >= MARGIN if j % 2 else at < LANES - MARGIN, here, there)

    width = 2 * PATCH
    for j in range(patches):
        at = slice(j * HALF, (j + 1) * HALF)
        for base, value in zip((0, width), parts):
            own = pick(value, j)
            left[at, base : base + PATCH] = own[:HALF]
            left[at, base + PATCH : base + width] = own[HALF:]
            if base == 0:
                left[at, 2 * width : 2 * width + PATCH] = own[:HALF]
                left[at, 2 * width + PATCH :] = own[HALF:]
    line = lax.broadcasted_iota(jnp.int32, (8, LANES), 0)
    gathered = jnp.zeros((8, LANES), F32)
    for j in range(patches):
        gathered = jnp.where(line == j, pick(middle, j), gathered)
    high, low = split(jnp.concatenate([gathered, jnp.zeros_like(gathered)]))
    at = slice(patches * HALF, patches * HALF + NYQ)
    blank = jnp.zeros((NYQ, PATCH), BF16)
    for base, value in zip((0, width, 2 * width), (high, low, high)):
        left[at, base : base + PATCH] = value
        left[at, base + PATCH : base + width] = blank


def spectra(pixels, rows, cols, left, out):
    for r, x in enumerate(pixels):
        expand(x, rows, left.at[r])
    for r in range(len(pixels)):
        out[r] = dot(left[r], cols[...])


def multiply(own, back, back_cols, half):
    size = own.shape[0]
    xr, xi = own[:, :PATCH], own[:, PATCH:]
    yr, yi = back[:, :PATCH], back[:, PATCH:]
    product = jnp.concatenate([xr * yr + xi * yi, xi * yr - xr * yi], 1)
    found = dot(jnp.concatenate(split(product)), back_cols[...])
    half[...] = (found[:size, :LANES] + found[size:, :LANES]) + (found[:size, LANES:] + found[size:, LANES:])


def stack(half, right):
    patches = (half.shape[0] - NYQ) // HALF
    high, low = split(half[: patches * HALF])
    for j in range(patches):
        at, lanes = slice(j * HALF, (j + 1) * HALF), slice(j * LANES, (j + 1) * LANES)
        for q, value in enumerate((high, low, high, low)):
            right[q * HALF : (q + 1) * HALF, lanes] = value[at]


def finish(half, back_rows, right, lagged):
    patches = (half.shape[0] - NYQ) // HALF
    middle = half[patches * HALF : patches * HALF + patches] * (1.0 / PATCH**3)
    found = dot(back_rows[...], right[...])
    lane = lax.broadcasted_iota(jnp.int32, (PAIRS, LANES), 1)
    for j in range(patches):
        lanes = slice(j * LANES, (j + 1) * LANES)
        cos_even, cos_odd, sin_even, sin_odd = (found[q * PAIRS : (q + 1) * PAIRS, lanes] for q in range(4))
        stay = jnp.where(lane < CROP, cos_even, sin_odd)
        move = jnp.where(lane < CROP, cos_odd, sin_even)
        lagged[pl.ds(j, PAIRS, stride=patches), :] = stay + pltpu.roll(move, CROP, 1)
    middle = jnp.where(lane[:patches] < CROP, middle, -pltpu.roll(middle, CROP, 1))
    return lagged[...].reshape(PAIRS, patches, LANES) + middle[None]


def surfaces(pixels, own, rows, cols, back_rows, back_cols, left, spec, half, right, lagged):
    spectra(pixels, rows, cols, left, spec)
    for r in range(len(pixels)):
        multiply(own(r), spec[r], back_cols, half.at[r])
    for r in range(len(pixels)):
        stack(half.at[r], right.at[r])
    return lambda r: finish(half.at[r], back_rows, right.at[r], lagged.at[r])


def own_kernel(at, mine, other, table, out, left, *_):
    rows, cols = table.at[at[0]], table.at[at[1]]
    lower = lax.axis_index("pln") == 1
    mine, other = mine[...], other[1 - lax.axis_index("pln")]
    spectra([outer_row(mine, lower)] + inner_rows(mine, other, lower), rows, cols, left, out)


def reached(distance, work):
    present = lax.axis_index("sec") >= distance
    pl.when(present)(lambda: work(True))
    pl.when(jnp.logical_not(present))(lambda: work(False))


def first_kernel(at, mine, both, own, table, out, *scratch):
    pln = lax.axis_index("pln")

    @pl.when(lax.rem(lax.axis_index("sec"), 2) == 1)
    def _():
        here, there = mine[...], both[1 - pln]
        pixels = [outer_row(here, pln == 1)] + inner_rows(here, there, pln == 1)[:1]
        found = surfaces(pixels, lambda r: own[r], *(table.at[x] for x in at), *scratch)
        for r in range(len(pixels)):
            out[r] = found(r)


def joined_row(one, two):
    joined = one + two + one * two
    patches = joined.shape[1]
    line = lax.broadcasted_iota(jnp.int32, joined.shape, 1)
    before = jnp.where(line == 0, 0.0, pltpu.roll(joined, 1, 1))
    after = jnp.where(line == patches - 1, 0.0, pltpu.roll(joined, patches - 1, 1))
    return (2.0 * joined + before + after) * (1.0 / 16.0)


def outer_kernel(at, mine, earlier, both, own, first, table, out, near, far, *scratch):
    pln, sec = lax.axis_index("pln"), lax.axis_index("sec")
    odd = lax.rem(sec, 2) == 1

    def found(two, one):
        outer = [outer_row(mine[...], pln == 1)] if two else []
        ahead = [outer_row(earlier[...], pln == 1)] + inner_rows(earlier[...], both[1 - pln], pln == 1)
        rows = ([0] if two else []) + one
        return surfaces(outer + [ahead[r] for r in one], lambda r: own[rows[r]], *[table.at[x] for x in at], *scratch)

    @pl.when(odd & (sec >= 2))
    def _():
        got = found(True, [2])
        out[...] = joined_row(first[0], got(0))
        near[...] = first[1]
        far[...] = got(1)

    @pl.when(jnp.logical_not(odd) & (sec >= 2))
    def _():
        got = found(True, [0, 1, 2])
        two = got(0)
        out[...] = joined_row(got(1), two)
        near[...] = got(2)
        far[...] = got(3)

    @pl.when(sec == 1)
    def _():
        one = first[0]
        out[...] = joined_row(one, jnp.zeros_like(one))
        near[...] = first[1]
        far[...] = found(False, [2])(0)

    @pl.when(sec == 0)
    def _():
        for x in (out, near, far):
            x[...] = jnp.zeros_like(x)


def inner_kernel(at, mine, other, own, outer, beside, beyond, table, out, left, spec, half, right, lagged, staged, sent):
    pln = lax.axis_index("pln")

    def send(slot, row, value):
        for pair in range(PAIRS):
            staged[slot, :, pair * LANES : (pair + 1) * LANES] = value[pair]
        copy = pltpu.make_async_copy(staged.at[slot], out.at[row], sent.at[slot])
        copy.start()
        return copy

    def work(present):
        found = lambda r: jnp.zeros(outer.shape, F32)
        if present:
            pixels = inner_rows(mine[...], other[...], pln == 1)
            parts = (table.at[x] for x in at)
            found = surfaces(pixels, lambda r: own[r + 1], *parts, left, spec, half, right, lagged)
        near = joined_row(beside[...], found(0))
        ending = outer[...]
        copies = [send(0, pln, 2.0 * ending + near)]
        far = joined_row(beyond[...], found(1))
        copies.append(send(1, 1 - pln, ending + 2.0 * near + far))
        for copy in copies:
            copy.wait()

    reached(2, work)


def from_sections(tile, distance, ring):
    count = lax.axis_size("sec")
    route = [(i, (i + distance) % count) for i in range(count) if ring or i + distance < count]
    return lax.ppermute(tile, "sec", route)


def sibling(tile):
    return lax.ppermute(tile, "pln", [(0, 1), (1, 0)])


def body(section_tiles):
    tile = section_tiles[0]
    height, width = tile.shape
    patches = width // STRIDE
    assert height == PATCH and lax.axis_size("pln") == 2 and patches == 8
    table, at = tables()
    packed = patches * HALF + NYQ
    shape = (PAIRS, patches, LANES)

    def call(kernel, shape, spread, *args, outs=1):
        scratch = [
            pltpu.VMEM((spread, packed, 6 * PATCH), BF16),
            pltpu.VMEM((spread, packed, 2 * PATCH), F32),
            pltpu.VMEM((spread, packed, LANES), F32),
            pltpu.VMEM((spread, 4 * HALF, patches * LANES), BF16),
            pltpu.VMEM((spread, PAIRS * patches, LANES), F32),
        ]
        ending = [pltpu.VMEM(shape, F32), pltpu.SemaphoreType.DMA((2,))] if kernel is inner_kernel else []
        return pl.pallas_call(
            functools.partial(kernel, at),
            out_shape=[jax.ShapeDtypeStruct(shape, F32)] * outs,
            out_specs=[pl.BlockSpec(memory_space=pl.ANY if ending else pltpu.VMEM)] * outs,
            scratch_shapes=scratch + ending,
            compiler_params=pltpu.CompilerParams(vmem_limit_bytes=40 * 2**20),
        )(*args)

    one_back = from_sections(tile, 1, True)
    two_back = from_sections(tile, 2, True)
    (own,) = call(own_kernel, (3, packed, 2 * PATCH), 3, tile, lax.all_gather(tile, "pln"), table)
    one_back, own = lax.optimization_barrier((one_back, own))
    both = lax.all_gather(one_back, "pln")
    (first,) = call(first_kernel, (2,) + shape, 2, one_back, both, own, table)
    two_back, first = lax.optimization_barrier((two_back, first))
    other = sibling(two_back)
    outer, beside, beyond = call(outer_kernel, shape, 4, two_back, one_back, both, own, first, table, outs=3)
    (mixed,) = call(inner_kernel, (2, patches, CROP * CROP), 2, two_back, other, own, outer, beside, beyond, table)
    return mixed[None]


def solution(mesh):
    placed = (P(("blocks", "sec"), "pln", None),)
    return jax.shard_map(
        body,
        mesh=mesh,
        in_specs=placed,
        out_specs=P(("blocks", "sec"), "pln", None, None),
        check_vma=False,
    )
```

```python
import functools

import jax
import jax.numpy as jnp
import numpy as np
from jax import lax
from jax.experimental import pallas as pl
from jax.experimental.pallas import tpu as pltpu
from jax.sharding import PartitionSpec as P

PATCH = 128
STRIDE = 64
CROP = 64
MARGIN = 32
HALF = PATCH // 2
LANES = 128
PAIRS = CROP // 2
NYQ = 16

BF16 = jnp.bfloat16
F32 = jnp.float32


def high_low(table):
    table = np.asarray(table, np.float32)
    high = table.astype(jnp.bfloat16)
    low = (table - high.astype(np.float32)).astype(jnp.bfloat16)
    return high, low


def tables():
    turn = 2.0 * np.pi / PATCH
    freq, place, full = np.arange(HALF), np.arange(PATCH), np.arange(PATCH)
    angle = turn * (np.outer(freq, place) % PATCH)
    high, low = high_low(np.concatenate([np.cos(angle), -np.sin(angle)]))
    middle = np.tile((-1.0) ** place, (NYQ, 1)).astype(jnp.bfloat16)
    nothing = np.zeros_like(high)
    rows = np.concatenate(
        [np.concatenate([high, high], 1), np.concatenate([middle, middle], 1), np.concatenate([low, nothing], 1)]
    )
    angle = turn * (np.outer(place, full) % PATCH)
    cos, sin = np.cos(angle), np.sin(angle)
    high, low = high_low(np.block([[cos, -sin], [sin, cos]]))
    cols = np.concatenate([high, high, low])
    lags = np.arange(CROP) - CROP // 2
    angle = turn * (np.outer(full, lags) % PATCH)
    cos, sin = np.cos(angle), np.sin(angle)
    high, low = high_low(np.block([[cos, sin], [-sin, cos]]))
    back_cols = np.concatenate([high, low], 1)
    ordered = np.concatenate([lags[0::2], lags[1::2]])
    weight = np.where(freq == 0, 1.0, 2.0) / PATCH**3
    angle = turn * (np.outer(ordered, freq) % PATCH)
    high, low = high_low(np.concatenate([np.cos(angle) * weight, -np.sin(angle) * weight]))
    back_rows = np.concatenate([high, high, low, low], 1)
    parts = (rows, cols, back_rows, back_cols)
    ends = np.cumsum([len(x) for x in parts])
    return np.concatenate(parts), [slice(int(end) - len(x), int(end)) for x, end in zip(parts, ends)]


def dot(left, right):
    return jnp.dot(left, right, preferred_element_type=F32)


def split(value):
    high = value.astype(BF16)
    return high, (value - high.astype(F32)).astype(BF16)


def outer_row(mine, lower):
    zero = jnp.zeros((MARGIN, mine.shape[1]), F32)
    first, last = mine[:MARGIN], mine[-MARGIN:]
    return jnp.concatenate([jnp.where(lower, zero, first), mine[MARGIN:-MARGIN], jnp.where(lower, last, zero)])


def inner_rows(mine, other, lower):
    first = jnp.where(lower, mine[:MARGIN], other[:MARGIN])
    last = jnp.where(lower, other[-MARGIN:], mine[-MARGIN:])
    return [jnp.concatenate([first, x[MARGIN:-MARGIN], last]) for x in (mine, other)]


def expand(pixels, rows, left):
    tiles = pixels.shape[1] // LANES
    patches = pixels.shape[1] // STRIDE
    found = dot(rows[...], jnp.concatenate(split(pixels)))
    parts = split(found[:PATCH] + found[PATCH + NYQ :])
    middle = found[PATCH : PATCH + 8]
    lane = lax.broadcasted_iota(jnp.int32, (PATCH, LANES), 1)

    def pick(value, j):
        tile = j // 2
        here = value[:, tile * LANES : (tile + 1) * LANES]
        beside = tile + 1 if j % 2 else tile - 1
        if 0 <= beside < tiles:
            there = value[:, beside * LANES : (beside + 1) * LANES]
        else:
            there = jnp.zeros_like(here)
        at = lane[: value.shape[0]]
        return jnp.where(at >= MARGIN if j % 2 else at < LANES - MARGIN, here, there)

    width = 2 * PATCH
    for j in range(patches):
        at = slice(j * HALF, (j + 1) * HALF)
        for base, value in zip((0, width), parts):
            own = pick(value, j)
            left[at, base : base + PATCH] = own[:HALF]
            left[at, base + PATCH : base + width] = own[HALF:]
            if base == 0:
                left[at, 2 * width : 2 * width + PATCH] = own[:HALF]
                left[at, 2 * width + PATCH :] = own[HALF:]
    line = lax.broadcasted_iota(jnp.int32, (8, LANES), 0)
    gathered = jnp.zeros((8, LANES), F32)
    for j in range(patches):
        gathered = jnp.where(line == j, pick(middle, j), gathered)
    high, low = split(jnp.concatenate([gathered, jnp.zeros_like(gathered)]))
    at = slice(patches * HALF, patches * HALF + NYQ)
    blank = jnp.zeros((NYQ, PATCH), BF16)
    for base, value in zip((0, width, 2 * width), (high, low, high)):
        left[at, base : base + PATCH] = value
        left[at, base + PATCH : base + width] = blank


def spectra(pixels, rows, cols, left, out):
    for r, x in enumerate(pixels):
        expand(x, rows, left.at[r])
    for r in range(len(pixels)):
        out[r] = dot(left[r], cols[...])


def multiply(own, back, back_cols, half):
    size = own.shape[0]
    xr, xi = own[:, :PATCH], own[:, PATCH:]
    yr, yi = back[:, :PATCH], back[:, PATCH:]
    product = jnp.concatenate([xr * yr + xi * yi, xi * yr - xr * yi], 1)
    found = dot(jnp.concatenate(split(product)), back_cols[...])
    half[...] = (found[:size, :LANES] + found[size:, :LANES]) + (found[:size, LANES:] + found[size:, LANES:])


def stack(half, right):
    patches = (half.shape[0] - NYQ) // HALF
    high, low = split(half[: patches * HALF])
    for j in range(patches):
        at, lanes = slice(j * HALF, (j + 1) * HALF), slice(j * LANES, (j + 1) * LANES)
        for q, value in enumerate((high, low, high, low)):
            right[q * HALF : (q + 1) * HALF, lanes] = value[at]


def finish(half, back_rows, right, lagged):
    patches = (half.shape[0] - NYQ) // HALF
    middle = half[patches * HALF : patches * HALF + patches] * (1.0 / PATCH**3)
    found = dot(back_rows[...], right[...])
    lane = lax.broadcasted_iota(jnp.int32, (PAIRS, LANES), 1)
    for j in range(patches):
        lanes = slice(j * LANES, (j + 1) * LANES)
        cos_even, cos_odd, sin_even, sin_odd = (found[q * PAIRS : (q + 1) * PAIRS, lanes] for q in range(4))
        stay = jnp.where(lane < CROP, cos_even, sin_odd)
        move = jnp.where(lane < CROP, cos_odd, sin_even)
        lagged[pl.ds(j, PAIRS, stride=patches), :] = stay + pltpu.roll(move, CROP, 1)
    middle = jnp.where(lane[:patches] < CROP, middle, -pltpu.roll(middle, CROP, 1))
    return lagged[...].reshape(PAIRS, patches, LANES) + middle[None]


def surfaces(pixels, own, rows, cols, back_rows, back_cols, left, spec, half, right, lagged):
    spectra(pixels, rows, cols, left, spec)
    for r in range(len(pixels)):
        multiply(own(r), spec[r], back_cols, half.at[r])
    for r in range(len(pixels)):
        stack(half.at[r], right.at[r])
    return lambda r: finish(half.at[r], back_rows, right.at[r], lagged.at[r])


def own_kernel(at, mine, other, table, out, left, *_):
    rows, cols = table.at[at[0]], table.at[at[1]]
    lower = lax.axis_index("pln") == 1
    mine, other = mine[...], other[1 - lax.axis_index("pln")]
    spectra([outer_row(mine, lower)] + inner_rows(mine, other, lower), rows, cols, left, out)


def reached(distance, work):
    present = lax.axis_index("sec") >= distance
    pl.when(present)(lambda: work(True))
    pl.when(jnp.logical_not(present))(lambda: work(False))


def first_kernel(at, mine, both, own, table, out, *scratch):
    pln = lax.axis_index("pln")

    @pl.when(lax.rem(lax.axis_index("sec"), 2) == 1)
    def _():
        here, there = mine[...], both[1 - pln]
        pixels = [outer_row(here, pln == 1)] + inner_rows(here, there, pln == 1)
        found = surfaces(pixels, lambda r: own[r], *(table.at[x] for x in at), *scratch)
        for r in range(len(pixels)):
            out[r] = found(r)


def joined_row(one, two):
    joined = one + two + one * two
    patches = joined.shape[1]
    line = lax.broadcasted_iota(jnp.int32, joined.shape, 1)
    before = jnp.where(line == 0, 0.0, pltpu.roll(joined, 1, 1))
    after = jnp.where(line == patches - 1, 0.0, pltpu.roll(joined, patches - 1, 1))
    return (2.0 * joined + before + after) * (1.0 / 16.0)


def outer_kernel(at, mine, earlier, both, own, first, table, out, near, far, *scratch):
    pln, sec = lax.axis_index("pln"), lax.axis_index("sec")
    odd = lax.rem(sec, 2) == 1

    def found(two, one):
        outer = [outer_row(mine[...], pln == 1)] if two else []
        ahead = [outer_row(earlier[...], pln == 1)] + inner_rows(earlier[...], both[1 - pln], pln == 1)
        rows = ([0] if two else []) + one
        return surfaces(outer + [ahead[r] for r in one], lambda r: own[rows[r]], *[table.at[x] for x in at], *scratch)

    @pl.when(odd & (sec >= 2))
    def _():
        out[...] = joined_row(first[0], found(True, [])(0))
        near[...] = first[1]
        far[...] = first[2]

    @pl.when(jnp.logical_not(odd) & (sec >= 2))
    def _():
        got = found(True, [0, 1, 2])
        two = got(0)
        out[...] = joined_row(got(1), two)
        near[...] = got(2)
        far[...] = got(3)

    @pl.when(sec == 1)
    def _():
        one = first[0]
        out[...] = joined_row(one, jnp.zeros_like(one))
        near[...] = first[1]
        far[...] = first[2]

    @pl.when(sec == 0)
    def _():
        for x in (out, near, far):
            x[...] = jnp.zeros_like(x)


def inner_kernel(at, mine, other, own, outer, beside, beyond, table, out, left, spec, half, right, lagged, staged, sent):
    pln = lax.axis_index("pln")

    def send(slot, row, value):
        for pair in range(PAIRS):
            staged[slot, :, pair * LANES : (pair + 1) * LANES] = value[pair]
        copy = pltpu.make_async_copy(staged.at[slot], out.at[row], sent.at[slot])
        copy.start()
        return copy

    def work(present):
        found = lambda r: jnp.zeros(outer.shape, F32)
        if present:
            pixels = inner_rows(mine[...], other[...], pln == 1)
            parts = (table.at[x] for x in at)
            found = surfaces(pixels, lambda r: own[r + 1], *parts, left, spec, half, right, lagged)
        near = joined_row(beside[...], found(0))
        ending = outer[...]
        copies = [send(0, pln, 2.0 * ending + near)]
        far = joined_row(beyond[...], found(1))
        copies.append(send(1, 1 - pln, ending + 2.0 * near + far))
        for copy in copies:
            copy.wait()

    reached(2, work)


def from_sections(tile, distance, ring):
    count = lax.axis_size("sec")
    route = [(i, (i + distance) % count) for i in range(count) if ring or i + distance < count]
    return lax.ppermute(tile, "sec", route)


def sibling(tile):
    return lax.ppermute(tile, "pln", [(0, 1), (1, 0)])


def body(section_tiles):
    tile = section_tiles[0]
    height, width = tile.shape
    patches = width // STRIDE
    assert height == PATCH and lax.axis_size("pln") == 2 and patches == 8
    table, at = tables()
    packed = patches * HALF + NYQ
    shape = (PAIRS, patches, LANES)

    def call(kernel, shape, spread, *args, outs=1):
        scratch = [
            pltpu.VMEM((spread, packed, 6 * PATCH), BF16),
            pltpu.VMEM((spread, packed, 2 * PATCH), F32),
            pltpu.VMEM((spread, packed, LANES), F32),
            pltpu.VMEM((spread, 4 * HALF, patches * LANES), BF16),
            pltpu.VMEM((spread, PAIRS * patches, LANES), F32),
        ]
        ending = [pltpu.VMEM(shape, F32), pltpu.SemaphoreType.DMA((2,))] if kernel is inner_kernel else []
        return pl.pallas_call(
            functools.partial(kernel, at),
            out_shape=[jax.ShapeDtypeStruct(shape, F32)] * outs,
            out_specs=[pl.BlockSpec(memory_space=pl.ANY if ending else pltpu.VMEM)] * outs,
            scratch_shapes=scratch + ending,
            compiler_params=pltpu.CompilerParams(vmem_limit_bytes=40 * 2**20),
        )(*args)

    one_back = from_sections(tile, 1, True)
    two_back = from_sections(tile, 2, True)
    (own,) = call(own_kernel, (3, packed, 2 * PATCH), 3, tile, lax.all_gather(tile, "pln"), table)
    one_back, own = lax.optimization_barrier((one_back, own))
    both = lax.all_gather(one_back, "pln")
    (first,) = call(first_kernel, (3,) + shape, 3, one_back, both, own, table)
    two_back, first = lax.optimization_barrier((two_back, first))
    other = sibling(two_back)
    outer, beside, beyond = call(outer_kernel, shape, 4, two_back, one_back, both, own, first, table, outs=3)
    (mixed,) = call(inner_kernel, (2, patches, CROP * CROP), 2, two_back, other, own, outer, beside, beyond, table)
    return mixed[None]


def solution(mesh):
    placed = (P(("blocks", "sec"), "pln", None),)
    return jax.shard_map(
        body,
        mesh=mesh,
        in_specs=placed,
        out_specs=P(("blocks", "sec"), "pln", None, None),
        check_vma=False,
    )
```
